32 devices in a mesh: leaf: 8 (over z, x), front: 4 (over y, core).
Axes of the slice: x: 2, y: 2, z: 4, core: 2. Of those that a mesh axis runs over, the one named last changes fastest.
Arguments:
- leaf_update: float32 [8192, 1024], P('leaf'), as said below
- separator_rows_1: float32 [2048, 1536], P(('leaf', 'front')), as said below
- remaining_rows_1: float32 [4096, 1536], P(('leaf', 'front'))
- separator_rows_2: float32 [1024, 1536], P(('leaf', 'front')), as said below
- remaining_rows_2: float32 [2048, 1536], P(('leaf', 'front'))
- separator_rows_3: float32 [512, 1536], P(('leaf', 'front')), as said below
- remaining_rows_3: float32 [1024, 1536], P(('leaf', 'front'))
- child_map_1: int32 [8, 8], replicated, may hold values from 0 to 11, as said below
- child_map_2: int32 [4, 8], replicated, may hold values from 0 to 11, as said below
- child_map_3: int32 [2, 8], replicated, may hold values from 0 to 11, as said below
Outputs:
- pivot_factor_1: float32 [2048, 512], P(('leaf', 'front'))
- below_factor_1: float32 [4096, 512], P(('leaf', 'front'))
- pivot_factor_2: float32 [1024, 512], P(('leaf', 'front'))
- below_factor_2: float32 [2048, 512], P(('leaf', 'front'))
- pivot_factor_3: float32 [512, 512], P(('leaf', 'front'))
- below_factor_3: float32 [1024, 512], P(('leaf', 'front'))
The draws below stay inside these ranges and needn't reach their ends.
Inputs may be any that keep to these rules, and one draw needn't show every extreme that they name: `child_map_1`: each row lists 8 distinct parent tiles in increasing order, the last one always 12 - 1. `child_map_2`: each row lists 8 distinct parent tiles in increasing order, the last one always 12 - 1. `child_map_3`: each row lists 8 distinct parent tiles in increasing order, the last one always 12 - 1. `leaf_update`: each block is symmetric positive definite, diagonal between 0.5 and 2, off-diagonal entries of magnitude about 0.008, smallest eigenvalue about 0.1 or more. Each front, separator_rows_1 above remaining_rows_1, is symmetric positive definite, diagonal between 2 and 4, off-diagonal entries of magnitude about 0.03, smallest eigenvalue about 0.35 or more. Each front, separator_rows_2 above remaining_rows_2, is symmetric positive definite, diagonal between 2 and 4, off-diagonal entries of magnitude about 0.03, smallest eigenvalue about 0.35 or more. Each front, separator_rows_3 above remaining_rows_3, is symmetric positive definite, diagonal between 2 and 4, off-diagonal entries of magnitude about 0.03, smallest eigenvalue about 0.35 or more.
All inputs are finite; a program needn't handle non-finite values.
Results may differ from the reference program's by a relative error of at most 0.0003.
Values sent between devices are 32-bit elements; how exact they have to be, the bound alone decides.
A program may use at most 128 MiB of HBM per device.

```python
import jax
import jax.numpy as jnp
from jax import lax

TILE = 128
SEP = 512
UPD = 1024
NF = 1536
NT = 12
UT = 8
N_LEAF = 8


def symmetric_fronts(key, front_total, order_size, spread, diag_low, diag_high):
    noise_key, diag_key, sign_key = jax.random.split(key, 3)
    noise_all = jax.random.normal(noise_key, (front_total, order_size, order_size), jnp.float32)
    diag_values = jax.random.uniform(diag_key, (front_total, order_size), jnp.float32, diag_low, diag_high)
    sign_draw = jax.random.randint(sign_key, (front_total, order_size), 0, 2)
    signs = (2 * sign_draw - 1).astype(jnp.float32)
    mirrored = (noise_all + jnp.swapaxes(noise_all, 1, 2)) * (spread * 0.70710678)
    coupled = mirrored + spread * signs[:, :, None] * signs[:, None, :]
    eye_mask = jnp.eye(order_size, dtype=jnp.float32)
    return coupled * (1.0 - eye_mask) + diag_values[:, :, None] * eye_mask


def draw_tile_map(key, row_total):
    random_bits = jax.random.randint(key, (row_total, NT - 1), 0, 1 << 20)
    scores = random_bits * NT + jnp.arange(NT - 1, dtype=jnp.int32)[None, :]
    picked = jnp.argsort(scores, axis=1)[:, :UT - 1]
    chosen = jnp.sort(picked, axis=1)
    last_tile = jnp.full((row_total, 1), NT - 1, dtype=jnp.int32)
    return jnp.concatenate([chosen.astype(jnp.int32), last_tile], axis=1).astype(jnp.int32)


def draw_leaf_update(key, part):
    fronts = symmetric_fronts(jax.random.fold_in(key, 21), N_LEAF, UPD, 0.006, 0.5, 2.0)
    return fronts.reshape(N_LEAF * UPD, UPD)


def draw_separator_rows_1(key, part):
    fronts = symmetric_fronts(jax.random.fold_in(key, 31), N_LEAF // 2, NF, 0.02, 2.0, 4.0)
    return fronts[:, :SEP].reshape(-1, NF)


def draw_remaining_rows_1(key, part):
    fronts = symmetric_fronts(jax.random.fold_in(key, 31), N_LEAF // 2, NF, 0.02, 2.0, 4.0)
    return fronts[:, SEP:].reshape(-1, NF)


def draw_separator_rows_2(key, part):
    fronts = symmetric_fronts(jax.random.fold_in(key, 32), N_LEAF // 4, NF, 0.02, 2.0, 4.0)
    return fronts[:, :SEP].reshape(-1, NF)


def draw_remaining_rows_2(key, part):
    fronts = symmetric_fronts(jax.random.fold_in(key, 32), N_LEAF // 4, NF, 0.02, 2.0, 4.0)
    return fronts[:, SEP:].reshape(-1, NF)


def draw_separator_rows_3(key, part):
    fronts = symmetric_fronts(jax.random.fold_in(key, 33), N_LEAF // 8, NF, 0.02, 2.0, 4.0)
    return fronts[:, :SEP].reshape(-1, NF)


def draw_remaining_rows_3(key, part):
    fronts = symmetric_fronts(jax.random.fold_in(key, 33), N_LEAF // 8, NF, 0.02, 2.0, 4.0)
    return fronts[:, SEP:].reshape(-1, NF)


def draw_child_map_1(key, part):
    return draw_tile_map(jax.random.fold_in(key, 41), N_LEAF)


def draw_child_map_2(key, part):
    return draw_tile_map(jax.random.fold_in(key, 42), N_LEAF // 2)


def draw_child_map_3(key, part):
    return draw_tile_map(jax.random.fold_in(key, 43), N_LEAF // 4)


def setup_inputs(seed: int = 0) -> dict:
    arg_keys = jax.random.split(jax.random.key(seed), 11)
    return {
        "leaf_update": draw_leaf_update(jax.random.fold_in(arg_keys[10], 71), 0),
        "separator_rows_1": draw_separator_rows_1(jax.random.fold_in(arg_keys[10], 71), 0),
        "remaining_rows_1": draw_remaining_rows_1(jax.random.fold_in(arg_keys[10], 71), 0),
        "separator_rows_2": draw_separator_rows_2(jax.random.fold_in(arg_keys[10], 71), 0),
        "remaining_rows_2": draw_remaining_rows_2(jax.random.fold_in(arg_keys[10], 71), 0),
        "separator_rows_3": draw_separator_rows_3(jax.random.fold_in(arg_keys[10], 71), 0),
        "remaining_rows_3": draw_remaining_rows_3(jax.random.fold_in(arg_keys[10], 71), 0),
        "child_map_1": draw_child_map_1(jax.random.fold_in(arg_keys[10], 71), 0),
        "child_map_2": draw_child_map_2(jax.random.fold_in(arg_keys[10], 71), 0),
        "child_map_3": draw_child_map_3(jax.random.fold_in(arg_keys[10], 71), 0),
    }


def tile_rows(tile_map):
    offsets = jnp.arange(TILE, dtype=jnp.int32)
    return (tile_map[:, None].astype(jnp.int32) * TILE + offsets[None, :]).reshape(-1).astype(jnp.int32)

def factor_front(sep_part, upd_part, first_child, second_child, first_map, second_map, with_update):
    front_full = jnp.concatenate([sep_part, upd_part], axis=0)
    for child_block, tile_map in ((first_child, first_map), (second_child, second_map)):
        index_list = tile_rows(tile_map)
        front_full = front_full.at[index_list[:, None], index_list[None, :]].add(child_block)
    diag_factor = jnp.linalg.cholesky(front_full[:SEP, :SEP])
    solved = lax.linalg.triangular_solve(diag_factor, front_full[SEP:, :SEP], left_side=False, lower=True, transpose_a=True)
    if with_update:
        update = front_full[SEP:, SEP:] - jnp.dot(solved, solved.T, precision=lax.Precision.HIGHEST)
        return (diag_factor, solved, update)
    return (diag_factor, solved)

def reference(leaf_update, separator_rows_1, remaining_rows_1, separator_rows_2, remaining_rows_2, separator_rows_3, remaining_rows_3, child_map_1, child_map_2, child_map_3):
    children = leaf_update.reshape(N_LEAF, UPD, UPD)
    sections = ((separator_rows_1, remaining_rows_1, child_map_1), (separator_rows_2, remaining_rows_2, child_map_2), (separator_rows_3, remaining_rows_3, child_map_3))
    outputs = []
    for section_number in range(1, 4):
        sep_all, upd_all, map_all = sections[section_number - 1]
        front_total = N_LEAF // 2 ** section_number
        with_update = section_number < 3

        def one_front(packed, with_update=with_update):
            sep_part, upd_part, pair_block, pair_maps = packed
            return factor_front(sep_part, upd_part, pair_block[0], pair_block[1], pair_maps[0], pair_maps[1], with_update)
        factors = lax.map(one_front, (sep_all.reshape(front_total, SEP, NF), upd_all.reshape(front_total, UPD, NF), children.reshape(front_total, 2, UPD, UPD), map_all.reshape(front_total, 2, UT)))
        outputs.append(factors[0].reshape(front_total * SEP, SEP))
        outputs.append(factors[1].reshape(front_total * UPD, SEP))
        if with_update:
            children = factors[2]
    return (outputs[0], outputs[1], outputs[2], outputs[3], outputs[4], outputs[5])
```

```python
import functools

import jax
import jax.numpy as jnp
from jax import lax
from jax.experimental import pallas as pl
from jax.experimental.pallas import tpu as pltpu
from jax.sharding import PartitionSpec as P

TILE = 128
SEP = 512
UPD = 1024
NF = 1536
NT = 12
UT = 8
STRIP = 8


def split(value):
    high = value.astype(jnp.bfloat16)
    return high, (value - high.astype(jnp.float32)).astype(jnp.bfloat16)


def dot3(left, right):
    def one(a, b):
        return lax.dot_general(a, b, (((1,), (1,)), ((), ())), preferred_element_type=jnp.float32)
    return one(left[0], right[0]) + (one(left[0], right[1]) + one(left[1], right[0]))


def invert_block(rows):
    count = len(rows)
    full = (STRIP, TILE)
    lane = lax.broadcasted_iota(jnp.int32, full, 1)
    sub = lax.broadcasted_iota(jnp.int32, full, 0)
    out = []
    for s in range(count):
        base = s * STRIP
        strip = rows[s]
        cols = [jnp.broadcast_to(strip[:, base + j:base + j + 1], full) for j in range(STRIP)]
        d = {(i, j): jnp.broadcast_to(cols[j][i:i + 1, :], full) for j in range(STRIP) for i in range(j, STRIP)}
        in_strip = (lane >= base) & (lane < base + STRIP)
        aug = jnp.where(in_strip, jnp.where(lane - base == sub, 1.0, 0.0), strip)
        x = [jnp.broadcast_to(aug[i:i + 1, :], full) for i in range(STRIP)]
        r = []
        for k in range(STRIP):
            r.append(lax.rsqrt(d[k, k]))
            for i in range(k + 1, STRIP):
                d[i, k] = d[i, k] * r[k]
            for j in range(k + 1, STRIP):
                for i in range(j, STRIP):
                    d[i, j] = d[i, j] - d[i, k] * d[j, k]
            x[k] = x[k] * r[k]
            for i in range(k + 1, STRIP):
                x[i] = x[i] - d[i, k] * x[k]
        u = x[0]
        for k in range(1, STRIP):
            u = jnp.where(sub == k, x[k], u)
        out.append(jnp.where(lane < base + STRIP, u, 0.0))
        if s == count - 1:
            break
        v = list(x)
        for k in range(STRIP - 1, -1, -1):
            v[k] = v[k] * r[k]
            for i in range(k):
                v[i] = v[i] - d[k, i] * v[k]
        for t in range(s + 1, count):
            row = rows[t]
            new = jnp.where(in_strip, 0.0, row)
            for j in range(STRIP):
                new = new - jnp.broadcast_to(row[:, base + j:base + j + 1], full) * v[j]
            rows[t] = new
    return out


def factor_block(b, panel, work, inv, high, low):
    total = panel.shape[0]
    start = pl.multiple_of(b * TILE, TILE)
    here = pl.ds(start, TILE)
    done = dot3((high[...], low[...]), (high[here, :], low[here, :]))
    work[...] = panel[:, here] - done
    strips = [work[pl.ds(pl.multiple_of(start + STRIP * t, STRIP), STRIP), :] for t in range(TILE // STRIP)]
    for t, strip in enumerate(invert_block(strips)):
        inv[STRIP * t:STRIP * t + STRIP, :] = strip
    column = dot3(split(work[...]), split(inv[...]))
    row_ids = lax.broadcasted_iota(jnp.int32, (total, TILE), 0)
    col_ids = lax.broadcasted_iota(jnp.int32, (total, TILE), 1) + start
    column = jnp.where(row_ids >= col_ids, column, 0.0)
    high_part, low_part = split(column)
    high[:, here] = high_part
    low[:, here] = low_part
    return column


def factor_kernel(pivot, below, diag, solved, panel, work, inv, high, low):
    panel[:SEP, :] = pivot[...]
    panel[SEP:, :] = below[...]
    high[...] = jnp.zeros_like(high)
    low[...] = jnp.zeros_like(low)

    @pl.loop(0, SEP // TILE)
    def _(b):
        column = factor_block(b, panel, work, inv, high, low)
        here = pl.ds(pl.multiple_of(b * TILE, TILE), TILE)
        diag[:, here] = column[:SEP]
        solved[:, here] = column[SEP:]


def factor(pivot, below):
    count = below.shape[0]
    total = SEP + count
    whole = pl.BlockSpec(memory_space=pltpu.VMEM)
    return pl.pallas_call(
        factor_kernel,
        out_shape=(
            jax.ShapeDtypeStruct((SEP, SEP), jnp.float32),
            jax.ShapeDtypeStruct((count, SEP), jnp.float32),
        ),
        in_specs=[whole, whole],
        out_specs=(whole, whole),
        scratch_shapes=[
            pltpu.VMEM((total, SEP), jnp.float32),
            pltpu.VMEM((total, TILE), jnp.float32),
            pltpu.VMEM((TILE, TILE), jnp.float32),
            pltpu.VMEM((total, SEP), jnp.bfloat16),
            pltpu.VMEM((total, SEP), jnp.bfloat16),
        ],
        compiler_params=pltpu.CompilerParams(vmem_limit_bytes=48 * 2**20),
    )(pivot, below)


def from_partner(block, axis, stride):
    count = lax.axis_size(axis)
    route = []
    for low in range(count):
        high = low | 1 << stride
        if high != low and high < count:
            route += [(low, high), (high, low)]
    return lax.ppermute(block, axis, route)


def collect(pieces, depth_count):
    gathered = lax.all_gather(pieces, "front", axis=0, tiled=True)
    leaf_place = lax.axis_index("leaf")
    for bit_number in range(depth_count):
        partner = from_partner(gathered, "leaf", bit_number)
        on_high = leaf_place >> bit_number & 1 == 1
        gathered = jnp.where(
            on_high,
            jnp.concatenate([partner, gathered], axis=0),
            jnp.concatenate([gathered, partner], axis=0),
        )
    return gathered


def owned_rows(position, group_count):
    sep_count = SEP // group_count
    upd_count = UPD // group_count
    sep_index = position * sep_count + jnp.arange(sep_count, dtype=jnp.int32)
    upd_index = SEP + position * upd_count + jnp.arange(upd_count, dtype=jnp.int32)
    return jnp.concatenate([sep_index, upd_index])


def locate(tile_map, targets):
    tile_of = targets // TILE
    offset = targets % TILE
    matches = tile_map[None, :] == tile_of[:, None]
    present = jnp.any(matches, axis=1)
    slot_ids = jnp.arange(tile_map.shape[0], dtype=jnp.int32)
    source = jnp.sum(jnp.where(matches, slot_ids[None, :], 0), axis=1)
    return (source * TILE + offset, present)


def select_rows(full_update, tile_map, targets):
    source, present = locate(tile_map, targets)
    return jnp.where(present[:, None], jnp.take(full_update, source, axis=0), 0.0)


def expand_columns(row_block, tile_map):
    placing = tile_map[:, None] == jnp.arange(NT, dtype=jnp.int32)[None, :]
    placed = []
    for n in range(NT):
        total = jnp.zeros((row_block.shape[0], TILE), jnp.float32)
        for u in range(UT):
            total = jnp.where(placing[u, n], row_block[:, u * TILE:(u + 1) * TILE], total)
        placed.append(total)
    return jnp.concatenate(placed, axis=1)


def body(
    leaf_update,
    separator_rows_1,
    remaining_rows_1,
    separator_rows_2,
    remaining_rows_2,
    separator_rows_3,
    remaining_rows_3,
    child_map_1,
    child_map_2,
    child_map_3,
):
    leaf_place = lax.axis_index("leaf")
    front_place = lax.axis_index("front")
    front_count = lax.axis_size("front")
    child_full = leaf_update
    sections = (
        (separator_rows_1, remaining_rows_1, child_map_1),
        (separator_rows_2, remaining_rows_2, child_map_2),
        (separator_rows_3, remaining_rows_3, child_map_3),
    )
    results = []
    for level_number in range(1, 4):
        sep_part, upd_part, child_maps = sections[level_number - 1]
        group_count = front_count * 2**level_number
        sep_count = SEP // group_count
        upd_count = UPD // group_count
        pair_bit = level_number - 1
        child_front = leaf_place >> pair_bit
        sibling_front = child_front ^ 1
        position = leaf_place % 2**level_number * front_count + front_place
        partner = (leaf_place ^ 1 << pair_bit) % 2**level_number * front_count + front_place
        own_map = lax.dynamic_index_in_dim(child_maps, child_front, 0, keepdims=False)
        sibling_map = lax.dynamic_index_in_dim(child_maps, sibling_front, 0, keepdims=False)
        targets = owned_rows(position, group_count)
        for_partner = select_rows(child_full, own_map, owned_rows(partner, group_count))
        sibling_block = from_partner(for_partner, "leaf", pair_bit)
        own_term = expand_columns(select_rows(child_full, own_map, targets), own_map)
        sibling_term = expand_columns(sibling_block, sibling_map)
        front_rows = jnp.concatenate([sep_part, upd_part], axis=0) + own_term + sibling_term
        if level_number < 3:
            panel_all = collect(front_rows[:, :SEP], level_number)
            blocks = panel_all.reshape(group_count, sep_count + upd_count, SEP)
            pivot_block = blocks[:, :sep_count].reshape(SEP, SEP)
            lower_block = blocks[:, sep_count:].reshape(UPD, SEP)
        else:
            pivot_block = collect(front_rows[:sep_count, :SEP], level_number)
            lower_block = front_rows[sep_count:, :SEP]
        diag_factor, solved_all = factor(pivot_block, lower_block)
        results.append(lax.dynamic_slice_in_dim(diag_factor, position * sep_count, sep_count, 0))
        if level_number < 3:
            solved_own = lax.dynamic_slice_in_dim(solved_all, position * upd_count, upd_count, 0)
            results.append(solved_own)
            update_own = front_rows[sep_count:, SEP:] - jnp.dot(
                solved_own, solved_all.T, precision=lax.Precision.HIGHEST
            )
            child_full = collect(update_own, level_number)
        else:
            results.append(solved_all)
    return tuple(results)


def solution(mesh):
    rows = P(("leaf", "front"), None)
    in_specs = (P("leaf", None),) + (rows,) * 6 + (P(),) * 3
    return jax.shard_map(body, mesh=mesh, in_specs=in_specs, out_specs=(rows,) * 6, check_vma=False)
```

```python
import functools

import jax
import jax.numpy as jnp
from jax import lax
from jax.experimental import pallas as pl
from jax.experimental.pallas import tpu as pltpu
from jax.sharding import PartitionSpec as P

TILE = 128
SEP = 512
UPD = 1024
NF = 1536
NT = 12
UT = 8
STRIP = 8
MESH = pl.DeviceIdType.MESH
WHOLE = pl.BlockSpec(memory_space=pltpu.VMEM)
SCALARS = pl.BlockSpec(memory_space=pltpu.SMEM)


def split(value):
    high = value.astype(jnp.bfloat16)
    return high, (value - high.astype(jnp.float32)).astype(jnp.bfloat16)


def dot3(left, right):
    def one(a, b):
        return lax.dot_general(a, b, (((1,), (1,)), ((), ())), preferred_element_type=jnp.float32)
    return one(left[0], right[0]) + (one(left[0], right[1]) + one(left[1], right[0]))


def invert_block(rows):
    count = len(rows)
    full = (STRIP, TILE)
    lane = lax.broadcasted_iota(jnp.int32, full, 1)
    sub = lax.broadcasted_iota(jnp.int32, full, 0)
    out = []
    for s in range(count):
        base = s * STRIP
        strip = rows[s]
        cols = [jnp.broadcast_to(strip[:, base + j:base + j + 1], full) for j in range(STRIP)]
        d = {(i, j): jnp.broadcast_to(cols[j][i:i + 1, :], full) for j in range(STRIP) for i in range(j, STRIP)}
        in_strip = (lane >= base) & (lane < base + STRIP)
        aug = jnp.where(in_strip, jnp.where(lane - base == sub, 1.0, 0.0), strip)
        x = [jnp.broadcast_to(aug[i:i + 1, :], full) for i in range(STRIP)]
        r = []
        for k in range(STRIP):
            r.append(lax.rsqrt(d[k, k]))
            for i in range(k + 1, STRIP):
                d[i, k] = d[i, k] * r[k]
            for j in range(k + 1, STRIP):
                for i in range(j, STRIP):
                    d[i, j] = d[i, j] - d[i, k] * d[j, k]
            x[k] = x[k] * r[k]
            for i in range(k + 1, STRIP):
                x[i] = x[i] - d[i, k] * x[k]
        u = x[0]
        for k in range(1, STRIP):
            u = jnp.where(sub == k, x[k], u)
        out.append(jnp.where(lane < base + STRIP, u, 0.0))
        if s == count - 1:
            break
        v = list(x)
        for k in range(STRIP - 1, -1, -1):
            v[k] = v[k] * r[k]
            for i in range(k):
                v[i] = v[i] - d[k, i] * v[k]
        for t in range(s + 1, count):
            row = rows[t]
            new = jnp.where(in_strip, 0.0, row)
            for j in range(STRIP):
                new = new - jnp.broadcast_to(row[:, base + j:base + j + 1], full) * v[j]
            rows[t] = new
    return out


def factor_block(b, pivot, below, work, inv, high, low):
    total = work.shape[0]
    start = pl.multiple_of(b * TILE, TILE)
    here = pl.ds(start, TILE)
    done = dot3((high[...], low[...]), (high[here, :], low[here, :]))
    work[:SEP, :] = pivot[:, here] - done[:SEP]
    work[SEP:, :] = below[:, here] - done[SEP:]
    strips = [work[pl.ds(pl.multiple_of(start + STRIP * t, STRIP), STRIP), :] for t in range(TILE // STRIP)]
    for t, strip in enumerate(invert_block(strips)):
        inv[STRIP * t:STRIP * t + STRIP, :] = strip
    column = dot3(split(work[...]), split(inv[...]))
    row_ids = lax.broadcasted_iota(jnp.int32, (total, TILE), 0)
    col_ids = lax.broadcasted_iota(jnp.int32, (total, TILE), 1) + start
    column = jnp.where(row_ids >= col_ids, column, 0.0)
    high_part, low_part = split(column)
    high[:, here] = high_part
    low[:, here] = low_part
    return column


def child_piece(table, row, count):
    tile = lax.div(row, jnp.int32(TILE))
    here = pl.multiple_of(table[tile] * TILE + lax.rem(row, jnp.int32(TILE)), 8)
    return here, table[NT + tile].astype(jnp.float32)


def spread(table, rows, here, count, present, n):
    there = pl.ds(pl.multiple_of(table[n] * TILE, TILE), TILE)
    return rows[pl.ds(here, count), there] * (present * table[NT + n].astype(jnp.float32))


def assemble(table, own, other, child_rows, sep, upd, own_sep, own_upd, out_sep, out_upd):
    for out, size, offset, place, entries in (
        (out_sep, sep.shape[0], 0, other, None),
        (own_sep, sep.shape[0], 0, own, sep),
        (out_upd, upd.shape[0], SEP, other, None),
        (own_upd, upd.shape[0], SEP, own, upd),
    ):
        here, present = child_piece(table, offset + place * size, size)
        rows, here = child_rows(here, size)
        for n in range(out.shape[1] // TILE):
            cols = slice(n * TILE, (n + 1) * TILE)
            value = spread(table, rows, here, size, present, n)
            out[:, cols] = value if entries is None else value + entries[:, cols]


def assemble_kernel(place, table, leaf, sep, upd, *outs):
    assemble(table, place[0], place[1], lambda here, size: (leaf, here), sep, upd, *outs)


def assembled_shapes(sep, upd, level):
    width = SEP if level == 3 else NF
    sep_shape = jax.ShapeDtypeStruct((sep.shape[0], SEP), jnp.float32)
    upd_shape = jax.ShapeDtypeStruct((upd.shape[0], width), jnp.float32)
    return [sep_shape, upd_shape, sep_shape, upd_shape]


def assemble_leaf(place, table, leaf, sep, upd):
    shapes = assembled_shapes(sep, upd, 1)
    return pl.pallas_call(
        assemble_kernel,
        out_shape=tuple(shapes),
        in_specs=[SCALARS] * 2 + [WHOLE] * 3,
        out_specs=(WHOLE,) * 4,
        compiler_params=pltpu.CompilerParams(vmem_limit_bytes=32 * 2**20),
    )(place, table, leaf, sep, upd)


def factor_kernel(with_update, place, pivot, below, *refs):
    if with_update:
        rest, table, sep, upd, diag, solved, *outs = refs
        outs, refs = outs[:4], outs[4:]
        full_diag, full_solved, work, inv, high, low, child = refs
    else:
        diag, solved, full_diag, full_solved, work, inv, high, low = refs
    high[...] = jnp.zeros_like(high)
    low[...] = jnp.zeros_like(low)

    @pl.loop(0, SEP // TILE)
    def _(b):
        column = factor_block(b, pivot, below, work, inv, high, low)
        here = pl.ds(pl.multiple_of(b * TILE, TILE), TILE)
        full_diag[:, here] = column[:SEP]
        full_solved[:, here] = column[SEP:]

    sep_count = diag.shape[0]
    diag[...] = full_diag[pl.ds(pl.multiple_of(place[0] * sep_count, 8), sep_count), :]
    if not with_update:
        solved[...] = full_solved[...]
        return
    upd_count = solved.shape[0]
    solved[...] = full_solved[pl.ds(pl.multiple_of(place[0] * upd_count, 8), upd_count), :]

    def update_rows(here, size):
        left = split(full_solved[pl.ds(here, size), :])
        child[:size, :] = rest[pl.ds(here, size), :] - dot3(left, (high[SEP:, :], low[SEP:, :]))
        return child, 0

    assemble(table, place[1], place[2], update_rows, sep, upd, *outs)


def factor(place, pivot, below, rest, sep_count, upd_count, level, following):
    count = below.shape[0]
    total = SEP + count
    out_shape = [
        jax.ShapeDtypeStruct((sep_count, SEP), jnp.float32),
        jax.ShapeDtypeStruct((upd_count, SEP), jnp.float32),
    ]
    operands = [place, pivot, below]
    specs = [SCALARS, WHOLE, WHOLE]
    scratch = [
        pltpu.VMEM((SEP, SEP), jnp.float32),
        pltpu.VMEM((count, SEP), jnp.float32),
        pltpu.VMEM((total, TILE), jnp.float32),
        pltpu.VMEM((TILE, TILE), jnp.float32),
        pltpu.VMEM((total, SEP), jnp.bfloat16),
        pltpu.VMEM((total, SEP), jnp.bfloat16),
    ]
    if rest is not None:
        table, sep, upd = following
        out_shape += assembled_shapes(sep, upd, level + 1)
        operands += [rest, table, sep, upd]
        specs += [WHOLE, SCALARS, WHOLE, WHOLE]
        scratch.append(pltpu.VMEM((upd.shape[0], UPD), jnp.float32))
    return pl.pallas_call(
        functools.partial(factor_kernel, rest is not None),
        out_shape=tuple(out_shape),
        in_specs=specs,
        out_specs=(WHOLE,) * len(out_shape),
        scratch_shapes=scratch,
        compiler_params=pltpu.CompilerParams(vmem_limit_bytes=48 * 2**20),
    )(*operands)


def bit_of(index, bit):
    return lax.rem(lax.div(index, jnp.int32(2**bit)), jnp.int32(2))


def front_dims(level, front_bits):
    return [("leaf", bit) for bit in range(level - 1, -1, -1)] + [("front", bit) for bit in range(front_bits - 1, -1, -1)]


def orders_of(level, front_bits):
    links = list(range(level + front_bits - 1))
    last = level + front_bits - 1
    if level == 3:
        swapped = links[:-2] + [links[-1], links[-2]]
        return [links + [last], swapped + [last]]
    return [links[turn:] + links[:turn] + [last] for turn in range(len(links))]


def column_parts(columns, parts):
    tiles = columns // TILE
    cuts = [round(tiles * part / parts) * TILE for part in range(parts + 1)]
    return [(cuts[part], cuts[part + 1] - cuts[part]) for part in range(parts)]


def partner_of(dim):
    axis, bit = dim
    index = lax.axis_index(axis)
    return {axis: index + (1 - 2 * bit_of(index, bit)) * 2**bit}


def doubling(buffer, dims, order, columns, send, recv):
    bits = [bit_of(lax.axis_index(axis), bit) for axis, bit in dims]
    copies = []
    for step, dim in enumerate(order):
        index = tuple(slice(None) if d in order[:step] else bits[d] for d in range(len(dims)))
        part = buffer.at[index + (slice(None), pl.ds(*columns))]
        copies.append(pltpu.make_async_remote_copy(
            src_ref=part,
            dst_ref=part,
            send_sem=send.at[step],
            recv_sem=recv.at[step],
            device_id=partner_of(dims[dim]),
            device_id_type=MESH,
        ))
    return copies


def exchange_kernel(level, front_bits, own_sep, own_upd, out_sep, out_upd, *refs):
    last = level == 3
    if last:
        f11, below = refs[:2]
        buffers = [f11]
        refs = refs[2:]
    else:
        f11, f21, f22 = refs[:3]
        buffers = [f11, f21, f22]
        refs = refs[3:]
    recv_sep, recv_upd, own_send, own_recv, all_send, all_recv = refs
    dims = front_dims(level, front_bits)
    bits = [bit_of(lax.axis_index(axis), bit) for axis, bit in dims]

    barrier = pltpu.get_barrier_semaphore()
    for dim in dims:
        pl.semaphore_signal(barrier, inc=1, device_id=partner_of(dim), device_id_type=MESH)
    pl.semaphore_wait(barrier, len(dims))

    def to_sibling(src, dst, slot):
        return pltpu.make_async_remote_copy(
            src_ref=src, dst_ref=dst, send_sem=own_send.at[slot], recv_sem=own_recv.at[slot],
            device_id=partner_of(dims[0]), device_id_type=MESH)

    sep_copy = to_sibling(out_sep, recv_sep, 0)
    upd_copy = to_sibling(out_upd, recv_upd, 1)
    sep_copy.start()
    upd_copy.start()

    chains = []
    for item, buffer in enumerate(buffers):
        orders = orders_of(level, front_bits)
        for part, columns in enumerate(column_parts(buffer.shape[-1], len(orders))):
            slot = item * len(orders) + part
            chains.append(doubling(buffer, dims, orders[part], columns, all_send.at[slot], all_recv.at[slot]))
    first = len(orders)
    own = tuple(bits)

    sep_copy.wait()
    f11[own] = own_sep[...] + recv_sep[...]
    for chain in chains[:first]:
        chain[0].start()
    upd_copy.wait()
    if last:
        below[...] = own_upd[...] + recv_upd[...]
    else:
        f21[own] = own_upd[:, :SEP] + recv_upd[:, :SEP]
        f22[own] = own_upd[:, SEP:] + recv_upd[:, SEP:]
    for chain in chains[first:]:
        chain[0].start()
    for step in range(len(dims)):
        for chain in chains:
            chain[step].wait()
            if step + 1 < len(dims):
                chain[step + 1].start()


def exchange(level, front_bits, own_sep, own_upd, out_sep, out_upd):
    last = level == 3
    sep_count, upd_count = own_sep.shape[0], own_upd.shape[0]
    lead = (2,) * (level + front_bits)
    width = SEP if last else NF
    shapes = [lead + (sep_count, SEP)]
    shapes += [(upd_count, SEP)] if last else [lead + (upd_count, SEP), lead + (upd_count, UPD)]
    chains = len(orders_of(level, front_bits)) * (1 if last else 3)
    steps = len(lead)
    return pl.pallas_call(
        functools.partial(exchange_kernel, level, front_bits),
        out_shape=tuple(jax.ShapeDtypeStruct(shape, jnp.float32) for shape in shapes),
        in_specs=[WHOLE] * 4,
        out_specs=(WHOLE,) * len(shapes),
        scratch_shapes=[
            pltpu.VMEM((sep_count, SEP), jnp.float32),
            pltpu.VMEM((upd_count, width), jnp.float32),
            pltpu.SemaphoreType.DMA((2,)),
            pltpu.SemaphoreType.DMA((2,)),
            pltpu.SemaphoreType.DMA((chains, steps)),
            pltpu.SemaphoreType.DMA((chains, steps)),
        ],
        compiler_params=pltpu.CompilerParams(
            collective_id=level, has_side_effects=True, vmem_limit_bytes=48 * 2**20),
    )(own_sep, own_upd, out_sep, out_upd)


def tile_table(tile_map):
    tiles = jnp.arange(NT, dtype=jnp.int32)
    match = tile_map[:, None] == tiles[None, :]
    place = jnp.sum(jnp.where(match, jnp.arange(UT, dtype=jnp.int32)[:, None], 0), axis=0)
    return jnp.concatenate([place, jnp.any(match, axis=0).astype(jnp.int32)])


def body(
    leaf_update,
    separator_rows_1,
    remaining_rows_1,
    separator_rows_2,
    remaining_rows_2,
    separator_rows_3,
    remaining_rows_3,
    child_map_1,
    child_map_2,
    child_map_3,
):
    leaf_place = lax.axis_index("leaf")
    front_place = lax.axis_index("front")
    front_count = lax.axis_size("front")
    front_bits = front_count.bit_length() - 1
    sections = (
        (separator_rows_1, remaining_rows_1, child_map_1),
        (separator_rows_2, remaining_rows_2, child_map_2),
        (separator_rows_3, remaining_rows_3, child_map_3),
    )
    tables = [
        tile_table(lax.dynamic_index_in_dim(maps, leaf_place >> number, 0, keepdims=False))
        for number, (_, _, maps) in enumerate(sections)
    ]
    positions = [
        (leaf_place % 2**level * front_count + front_place, (leaf_place ^ 1 << level - 1) % 2**level * front_count + front_place)
        for level in range(1, 4)
    ]
    results = []
    sep, upd, _ = sections[0]
    rows = assemble_leaf(jnp.stack(positions[0]).astype(jnp.int32), tables[0], leaf_update, sep, upd)
    for level in range(1, 4):
        sep, upd, _ = sections[level - 1]
        parts = exchange(level, front_bits, *rows)
        pivot = parts[0].reshape(SEP, SEP)
        place = [positions[level - 1][0]]
        following = None
        if level < 3:
            below, rest = parts[1].reshape(UPD, SEP), parts[2].reshape(UPD, UPD)
            following = (tables[level],) + sections[level][:2]
            place += positions[level]
        else:
            below, rest = parts[1], None
        place = jnp.stack(place).astype(jnp.int32)
        outs = factor(place, pivot, below, rest, sep.shape[0], upd.shape[0], level, following)
        results += outs[:2]
        rows = outs[2:]
    return tuple(results)


def solution(mesh):
    rows = P(("leaf", "front"), None)
    in_specs = (P("leaf", None),) + (rows,) * 6 + (P(),) * 3
    return jax.shard_map(body, mesh=mesh, in_specs=in_specs, out_specs=(rows,) * 6, check_vma=False)
```

```python
import functools

import jax
import jax.numpy as jnp
from jax import lax
from jax.experimental import pallas as pl
from jax.experimental.pallas import tpu as pltpu
from jax.sharding import PartitionSpec as P

TILE = 128
SEP = 512
UPD = 1024
NF = 1536
NT = 12
UT = 8
STRIP = 8
MESH = pl.DeviceIdType.MESH
WHOLE = pl.BlockSpec(memory_space=pltpu.VMEM)
SCALARS = pl.BlockSpec(memory_space=pltpu.SMEM)


def split(value):
    high = value.astype(jnp.bfloat16)
    return high, (value - high.astype(jnp.float32)).astype(jnp.bfloat16)


def dot3(left, right):
    def one(a, b):
        return lax.dot_general(a, b, (((1,), (1,)), ((), ())), preferred_element_type=jnp.float32)
    return one(left[0], right[0]) + (one(left[0], right[1]) + one(left[1], right[0]))


def invert_block(rows):
    count = len(rows)
    full = (STRIP, TILE)
    lane = lax.broadcasted_iota(jnp.int32, full, 1)
    sub = lax.broadcasted_iota(jnp.int32, full, 0)
    out = []
    for s in range(count):
        base = s * STRIP
        strip = rows[s]
        cols = [jnp.broadcast_to(strip[:, base + j:base + j + 1], full) for j in range(STRIP)]
        d = {(i, j): jnp.broadcast_to(cols[j][i:i + 1, :], full) for j in range(STRIP) for i in range(j, STRIP)}
        in_strip = (lane >= base) & (lane < base + STRIP)
        aug = jnp.where(in_strip, jnp.where(lane - base == sub, 1.0, 0.0), strip)
        x = [jnp.broadcast_to(aug[i:i + 1, :], full) for i in range(STRIP)]
        r = []
        for k in range(0, STRIP, 2):
            n = k + 1
            det = d[k, k] * d[n, n] - d[n, k] * d[n, k]
            r.append(lax.rsqrt(d[k, k]))
            r.append(d[k, k] * r[k] * lax.rsqrt(det))
            d[n, k] = d[n, k] * r[k]
            for i in range(k + 2, STRIP):
                d[i, k] = d[i, k] * r[k]
                d[i, n] = (d[i, n] - d[i, k] * d[n, k]) * r[n]
            for j in range(k + 2, STRIP):
                for i in range(j, STRIP):
                    d[i, j] = d[i, j] - (d[i, k] * d[j, k] + d[i, n] * d[j, n])
            x[k] = x[k] * r[k]
            x[n] = (x[n] - d[n, k] * x[k]) * r[n]
            for i in range(k + 2, STRIP):
                x[i] = x[i] - (d[i, k] * x[k] + d[i, n] * x[n])
        u = x[0]
        for k in range(1, STRIP):
            u = jnp.where(sub == k, x[k], u)
        out.append(jnp.where(lane < base + STRIP, u, 0.0))
        if s == count - 1:
            break
        v = list(x)
        for k in range(STRIP - 1, -1, -1):
            v[k] = v[k] * r[k]
            for i in range(k):
                v[i] = v[i] - d[k, i] * v[k]
        for t in range(s + 1, count):
            row = rows[t]
            new = jnp.where(in_strip, 0.0, row)
            for j in range(STRIP):
                new = new - jnp.broadcast_to(row[:, base + j:base + j + 1], full) * v[j]
            rows[t] = new
    return out


def pivot_block(b, pivot, diag, work, inv, high, low):
    start = pl.multiple_of(b * TILE, TILE)
    here = pl.ds(start, TILE)
    work[...] = pivot(here) - dot3((high[...], low[...]), (high[here, :], low[here, :]))
    strips = [work[pl.ds(pl.multiple_of(start + STRIP * t, STRIP), STRIP), :] for t in range(TILE // STRIP)]
    for t, strip in enumerate(invert_block(strips)):
        inv[b, STRIP * t:STRIP * t + STRIP, :] = strip
    column = dot3(split(work[...]), split(inv[b]))
    row_ids = lax.broadcasted_iota(jnp.int32, (SEP, TILE), 0)
    col_ids = lax.broadcasted_iota(jnp.int32, (SEP, TILE), 1) + start
    column = jnp.where(row_ids >= col_ids, column, 0.0)
    diag[:, here] = column
    high[:, here], low[:, here] = split(column)


def solve_block(b, below, solved, inv, high, low, done_high, done_low):
    here = pl.ds(pl.multiple_of(b * TILE, TILE), TILE)
    rest = below(here) - dot3((done_high[...], done_low[...]), (high[here, :], low[here, :]))
    column = dot3(split(rest), split(inv[b]))
    solved[:, here] = column
    done_high[:, here], done_low[:, here] = split(column)


def child_piece(table, row, count):
    tile = lax.div(row, jnp.int32(TILE))
    here = pl.multiple_of(table[tile] * TILE + lax.rem(row, jnp.int32(TILE)), 8)
    return here, table[NT + tile].astype(jnp.float32)


def spread(table, rows, here, count, present, n):
    there = pl.ds(pl.multiple_of(table[n] * TILE, TILE), TILE)
    return rows[pl.ds(here, count), there] * (present * table[NT + n].astype(jnp.float32))


def assemble(table, own, other, child_rows, sep, upd, own_sep, own_upd, out_sep, out_upd):
    for out, size, offset, place, entries in (
        (out_sep, sep.shape[0], 0, other, None),
        (own_sep, sep.shape[0], 0, own, sep),
        (out_upd, upd.shape[0], SEP, other, None),
        (own_upd, upd.shape[0], SEP, own, upd),
    ):
        here, present = child_piece(table, offset + place * size, size)
        rows, here = child_rows(here, size)
        for n in range(out.shape[1] // TILE):
            cols = slice(n * TILE, (n + 1) * TILE)
            value = spread(table, rows, here, size, present, n)
            out[:, cols] = value if entries is None else value + entries[:, cols]


def assemble_kernel(place, table, leaf, sep, upd, *outs):
    assemble(table, place[0], place[1], lambda here, size: (leaf, here), sep, upd, *outs)


def assembled_shapes(sep, upd, level):
    width = SEP if level == 3 else NF
    sep_shape = jax.ShapeDtypeStruct((sep.shape[0], SEP), jnp.float32)
    upd_shape = jax.ShapeDtypeStruct((upd.shape[0], width), jnp.float32)
    return [sep_shape, upd_shape, sep_shape, upd_shape]


def assemble_leaf(place, table, leaf, sep, upd):
    shapes = assembled_shapes(sep, upd, 1)
    return pl.pallas_call(
        assemble_kernel,
        out_shape=tuple(shapes),
        in_specs=[SCALARS] * 2 + [WHOLE] * 3,
        out_specs=(WHOLE,) * 4,
        compiler_params=pltpu.CompilerParams(vmem_limit_bytes=32 * 2**20),
    )(place, table, leaf, sep, upd)


def update_kernel(place, table, solved, rest, sep, upd, *refs):
    outs, (high, low, child) = refs[:4], refs[4:]
    high[...], low[...] = split(solved[...])

    def update_rows(here, size):
        left = split(solved[pl.ds(here, size), :])
        child[:size, :] = rest[pl.ds(here, size), :] - dot3(left, (high[...], low[...]))
        return child, 0

    assemble(table, place[0], place[1], update_rows, sep, upd, *outs)


def update(place, table, solved, rest, sep, upd, level):
    shapes = assembled_shapes(sep, upd, level)
    return pl.pallas_call(
        update_kernel,
        out_shape=tuple(shapes),
        in_specs=[SCALARS] * 2 + [WHOLE] * 4,
        out_specs=(WHOLE,) * 4,
        scratch_shapes=[
            pltpu.VMEM((UPD, SEP), jnp.bfloat16),
            pltpu.VMEM((UPD, SEP), jnp.bfloat16),
            pltpu.VMEM((upd.shape[0], UPD), jnp.float32),
        ],
        compiler_params=pltpu.CompilerParams(vmem_limit_bytes=40 * 2**20),
    )(place, table, solved, rest, sep, upd)


def bit_of(index, bit):
    return lax.rem(lax.div(index, jnp.int32(2**bit)), jnp.int32(2))


def front_dims(level, front_bits):
    return [("leaf", bit) for bit in range(level - 1, -1, -1)] + [("front", bit) for bit in range(front_bits - 1, -1, -1)]


def orders_of(level, front_bits):
    links = list(range(level + front_bits - 1))
    last = level + front_bits - 1
    if level == 3:
        swapped = links[:-2] + [links[-1], links[-2]]
        return [links + [last], swapped + [last]]
    return [links[turn:] + links[:turn] + [last] for turn in range(len(links))]


def column_parts(columns, parts):
    tiles = columns // TILE
    cuts = [round(tiles * part / parts) * TILE for part in range(parts + 1)]
    return [(cuts[part], cuts[part + 1] - cuts[part]) for part in range(parts)]


def partner_of(dim):
    axis, bit = dim
    index = lax.axis_index(axis)
    return {axis: index + (1 - 2 * bit_of(index, bit)) * 2**bit}


def doubling(buffer, dims, order, columns, send, recv):
    bits = [bit_of(lax.axis_index(axis), bit) for axis, bit in dims]
    copies = []
    for step, dim in enumerate(order):
        index = tuple(slice(None) if d in order[:step] else bits[d] for d in range(len(dims)))
        part = buffer.at[index + (slice(None), pl.ds(*columns))]
        copies.append(pltpu.make_async_remote_copy(
            src_ref=part,
            dst_ref=part,
            send_sem=send.at[step],
            recv_sem=recv.at[step],
            device_id=partner_of(dims[dim]),
            device_id_type=MESH,
        ))
    return copies


def level_kernel(level, front_bits, own_sep, own_upd, out_sep, out_upd, *refs):
    last = level == 3
    if last:
        diag, solved, below, full_solved, *refs = refs
    else:
        diag, solved, full_solved, f22, f21, *refs = refs
    f11, full_diag, work, inv, high, low, done_high, done_low, *refs = refs
    recv_sep, recv_upd, own_send, own_recv, all_send, all_recv = refs
    buffers = [f11] if last else [f11, f21, f22]
    dims = front_dims(level, front_bits)
    bits = [bit_of(lax.axis_index(axis), bit) for axis, bit in dims]
    steps = len(dims)
    position = lax.rem(lax.axis_index("leaf"), jnp.int32(2**level)) * 2**front_bits + lax.axis_index("front")

    barrier = pltpu.get_barrier_semaphore()
    for dim in dims:
        pl.semaphore_signal(barrier, inc=1, device_id=partner_of(dim), device_id_type=MESH)
    pl.semaphore_wait(barrier, steps)

    def to_sibling(src, dst, slot):
        return pltpu.make_async_remote_copy(
            src_ref=src, dst_ref=dst, send_sem=own_send.at[slot], recv_sem=own_recv.at[slot],
            device_id=partner_of(dims[0]), device_id_type=MESH)

    sep_copy = to_sibling(out_sep, recv_sep, 0)
    upd_copy = to_sibling(out_upd, recv_upd, 1)
    sep_copy.start()
    high[...] = jnp.zeros_like(high)
    low[...] = jnp.zeros_like(low)
    done_high[...] = jnp.zeros_like(done_high)
    done_low[...] = jnp.zeros_like(done_low)

    chains = []
    orders = orders_of(level, front_bits)
    for item, buffer in enumerate(buffers):
        for part, columns in enumerate(column_parts(buffer.shape[-1], len(orders))):
            slot = item * len(orders) + part
            chains.append(doubling(buffer, dims, orders[part], columns, all_send.at[slot], all_recv.at[slot]))
    early, late = chains[:len(orders)], chains[len(orders):]
    own = tuple(bits)

    def advance(which, step):
        for chain in which:
            if step >= 0:
                chain[step].wait()
            if step + 1 < steps:
                chain[step + 1].start()

    sep_copy.wait()
    f11[own] = own_sep[...] + recv_sep[...]
    advance(early, -1)
    for step in range(steps):
        if step == steps - 1:
            upd_copy.start()
        advance(early, step)

    def arrived():
        upd_copy.wait()
        if last:
            below[...] = own_upd[...] + recv_upd[...]
        else:
            f21[own] = own_upd[:, :SEP] + recv_upd[:, :SEP]
            f22[own] = own_upd[:, SEP:] + recv_upd[:, SEP:]
            advance(late, -1)

    blocks = SEP // TILE
    flat = (slice(None),) * len(dims)

    @pl.loop(0, blocks)
    def _(b):
        pivot_block(b, lambda here: f11[flat + (slice(None), here)].reshape(SEP, TILE), full_diag, work, inv, high, low)

        @pl.when(b == 0)
        def _():
            arrived()

        if not last:
            for step in range(steps - 1):
                @pl.when(b == blocks - steps + 1 + step)
                def _():
                    advance(late, step)

    for chain in late[:len(orders)]:
        chain[steps - 1].wait()

    @pl.loop(0, blocks)
    def _(b):
        if last:
            piece = lambda here: below[:, here]
        else:
            piece = lambda here: f21[flat + (slice(None), here)].reshape(UPD, TILE)
        solve_block(b, piece, full_solved, inv, high, low, done_high, done_low)

    sep_count, upd_count = diag.shape[0], solved.shape[0]
    diag[...] = full_diag[pl.ds(pl.multiple_of(position * sep_count, 8), sep_count), :]
    if last:
        solved[...] = full_solved[...]
    else:
        solved[...] = full_solved[pl.ds(pl.multiple_of(position * upd_count, 8), upd_count), :]
    for chain in late[len(orders):]:
        chain[steps - 1].wait()


def factor_level(level, front_bits, own_sep, own_upd, out_sep, out_upd):
    last = level == 3
    sep_count, upd_count = own_sep.shape[0], own_upd.shape[0]
    lead = (2,) * (level + front_bits)
    steps = len(lead)
    rows = upd_count if last else UPD
    shapes = [(sep_count, SEP), (upd_count, SEP)]
    scratch = [(upd_count, SEP), (upd_count, SEP)] if last else [lead + (upd_count, SEP)]
    if not last:
        shapes += [(UPD, SEP), lead + (upd_count, UPD)]
    scratch += [lead + (sep_count, SEP), (SEP, SEP), (SEP, TILE), (SEP // TILE, TILE, TILE)]
    halves = [(SEP, SEP)] * 2 + [(rows, SEP)] * 2
    received = [own_sep.shape, own_upd.shape]
    chains = len(orders_of(level, front_bits)) * (1 if last else 3)
    return pl.pallas_call(
        functools.partial(level_kernel, level, front_bits),
        out_shape=tuple(jax.ShapeDtypeStruct(shape, jnp.float32) for shape in shapes),
        in_specs=[WHOLE] * 4,
        out_specs=(WHOLE,) * len(shapes),
        scratch_shapes=[pltpu.VMEM(shape, jnp.float32) for shape in scratch]
        + [pltpu.VMEM(shape, jnp.bfloat16) for shape in halves]
        + [pltpu.VMEM(shape, jnp.float32) for shape in received]
        + [
            pltpu.SemaphoreType.DMA((2,)),
            pltpu.SemaphoreType.DMA((2,)),
            pltpu.SemaphoreType.DMA((chains, steps)),
            pltpu.SemaphoreType.DMA((chains, steps)),
        ],
        compiler_params=pltpu.CompilerParams(
            collective_id=level, has_side_effects=True, vmem_limit_bytes=48 * 2**20),
    )(own_sep, own_upd, out_sep, out_upd)


def tile_table(tile_map):
    tiles = jnp.arange(NT, dtype=jnp.int32)
    match = tile_map[:, None] == tiles[None, :]
    place = jnp.sum(jnp.where(match, jnp.arange(UT, dtype=jnp.int32)[:, None], 0), axis=0)
    return jnp.concatenate([place, jnp.any(match, axis=0).astype(jnp.int32)])


def body(
    leaf_update,
    separator_rows_1,
    remaining_rows_1,
    separator_rows_2,
    remaining_rows_2,
    separator_rows_3,
    remaining_rows_3,
    child_map_1,
    child_map_2,
    child_map_3,
):
    leaf_place = lax.axis_index("leaf")
    front_place = lax.axis_index("front")
    front_count = lax.axis_size("front")
    front_bits = front_count.bit_length() - 1
    sections = (
        (separator_rows_1, remaining_rows_1, child_map_1),
        (separator_rows_2, remaining_rows_2, child_map_2),
        (separator_rows_3, remaining_rows_3, child_map_3),
    )
    tables = [
        tile_table(lax.dynamic_index_in_dim(maps, leaf_place >> number, 0, keepdims=False))
        for number, (_, _, maps) in enumerate(sections)
    ]
    positions = [
        (leaf_place % 2**level * front_count + front_place, (leaf_place ^ 1 << level - 1) % 2**level * front_count + front_place)
        for level in range(1, 4)
    ]
    results = []
    sep, upd, _ = sections[0]
    rows = assemble_leaf(jnp.stack(positions[0]).astype(jnp.int32), tables[0], leaf_update, sep, upd)
    for level in range(1, 4):
        outs = factor_level(level, front_bits, *rows)
        results += outs[:2]
        if level < 3:
            place = jnp.stack(positions[level]).astype(jnp.int32)
            sep, upd, _ = sections[level]
            rows = update(place, tables[level], outs[2], outs[3].reshape(UPD, UPD), sep, upd, level + 1)
    return tuple(results)


def solution(mesh):
    rows = P(("leaf", "front"), None)
    in_specs = (P("leaf", None),) + (rows,) * 6 + (P(),) * 3
    return jax.shard_map(body, mesh=mesh, in_specs=in_specs, out_specs=(rows,) * 6, check_vma=False)
```

```python
import functools

import jax
import jax.numpy as jnp
from jax import lax
from jax.experimental import pallas as pl
from jax.experimental.pallas import tpu as pltpu
from jax.sharding import PartitionSpec as P

TILE = 128
SEP = 512
UPD = 1024
NF = 1536
NT = 12
UT = 8
STRIP = 8
MESH = pl.DeviceIdType.MESH
WHOLE = pl.BlockSpec(memory_space=pltpu.VMEM)
SCALARS = pl.BlockSpec(memory_space=pltpu.SMEM)


def split(value):
    high = value.astype(jnp.bfloat16)
    return high, (value - high.astype(jnp.float32)).astype(jnp.bfloat16)


def dot3(left, right):
    def one(a, b):
        return lax.dot_general(a, b, (((1,), (1,)), ((), ())), preferred_element_type=jnp.float32)
    return one(left[0], right[0]) + (one(left[0], right[1]) + one(left[1], right[0]))


def invert_block(rows):
    count = len(rows)
    full = (STRIP, TILE)
    lane = lax.broadcasted_iota(jnp.int32, full, 1)
    sub = lax.broadcasted_iota(jnp.int32, full, 0)
    out = []
    for s in range(count):
        base = s * STRIP
        strip = rows[s]
        cols = [jnp.broadcast_to(strip[:, base + j:base + j + 1], full) for j in range(STRIP)]
        d = {(i, j): jnp.broadcast_to(cols[j][i:i + 1, :], full) for j in range(STRIP) for i in range(j, STRIP)}
        in_strip = (lane >= base) & (lane < base + STRIP)
        aug = jnp.where(in_strip, jnp.where(lane - base == sub, 1.0, 0.0), strip)
        x = [jnp.broadcast_to(aug[i:i + 1, :], full) for i in range(STRIP)]
        r = []
        for k in range(0, STRIP, 2):
            n = k + 1
            det = d[k, k] * d[n, n] - d[n, k] * d[n, k]
            r.append(lax.rsqrt(d[k, k]))
            r.append(d[k, k] * r[k] * lax.rsqrt(det))
            d[n, k] = d[n, k] * r[k]
            for i in range(k + 2, STRIP):
                d[i, k] = d[i, k] * r[k]
                d[i, n] = (d[i, n] - d[i, k] * d[n, k]) * r[n]
            for j in range(k + 2, STRIP):
                for i in range(j, STRIP):
                    d[i, j] = d[i, j] - (d[i, k] * d[j, k] + d[i, n] * d[j, n])
            x[k] = x[k] * r[k]
            x[n] = (x[n] - d[n, k] * x[k]) * r[n]
            for i in range(k + 2, STRIP):
                x[i] = x[i] - (d[i, k] * x[k] + d[i, n] * x[n])
        u = x[0]
        for k in range(1, STRIP):
            u = jnp.where(sub == k, x[k], u)
        out.append(jnp.where(lane < base + STRIP, u, 0.0))
        if s == count - 1:
            break
        v = list(x)
        for k in range(STRIP - 1, -1, -1):
            v[k] = v[k] * r[k]
            for i in range(k):
                v[i] = v[i] - d[k, i] * v[k]
        for t in range(s + 1, count):
            row = rows[t]
            new = jnp.where(in_strip, 0.0, row)
            for j in range(STRIP):
                new = new - jnp.broadcast_to(row[:, base + j:base + j + 1], full) * v[j]
            rows[t] = new
    return out


def pivot_block(b, pivot, diag, work, inv, high, low):
    start = pl.multiple_of(b * TILE, TILE)
    here = pl.ds(start, TILE)
    work[...] = pivot(here) - dot3((high[...], low[...]), (high[here, :], low[here, :]))
    strips = [work[pl.ds(pl.multiple_of(start + STRIP * t, STRIP), STRIP), :] for t in range(TILE // STRIP)]
    for t, strip in enumerate(invert_block(strips)):
        inv[b, STRIP * t:STRIP * t + STRIP, :] = strip
    column = dot3(split(work[...]), split(inv[b]))
    row_ids = lax.broadcasted_iota(jnp.int32, (SEP, TILE), 0)
    col_ids = lax.broadcasted_iota(jnp.int32, (SEP, TILE), 1) + start
    column = jnp.where(row_ids >= col_ids, column, 0.0)
    diag[:, here] = column
    high[:, here], low[:, here] = split(column)


def solve_block(b, below, solved, inv, high, low, done_high, done_low):
    here = pl.ds(pl.multiple_of(b * TILE, TILE), TILE)
    rest = below(here) - dot3((done_high[...], done_low[...]), (high[here, :], low[here, :]))
    column = dot3(split(rest), split(inv[b]))
    solved[:, here] = column
    done_high[:, here], done_low[:, here] = split(column)


def child_piece(table, row, count):
    tile = lax.div(row, jnp.int32(TILE))
    here = pl.multiple_of(table[tile] * TILE + lax.rem(row, jnp.int32(TILE)), 8)
    return here, table[NT + tile].astype(jnp.float32)


def spread(table, rows, here, count, present, n):
    there = pl.ds(pl.multiple_of(table[n] * TILE, TILE), TILE)
    return rows[pl.ds(here, count), there] * (present * table[NT + n].astype(jnp.float32))


def assemble(table, own, other, child, finish, sep, upd, own_sep, own_upd, out_sep, out_upd, staged, sems):
    plan = (
        (out_sep, sep.shape[0], 0, other, None),
        (own_sep, sep.shape[0], 0, own, sep),
        (out_upd, upd.shape[0], SEP, other, None),
        (own_upd, upd.shape[0], SEP, own, upd),
    )
    pieces = []
    for number, (out, size, offset, place, entries) in enumerate(plan):
        here, present = child_piece(table, offset + place * size, size)
        copy = pltpu.make_async_copy(child.at[pl.ds(here, size), :], staged.at[number, pl.ds(0, size), :], sems.at[number])
        copy.start()
        pieces.append((here, present, copy))
    for number, (out, size, offset, place, entries) in enumerate(plan):
        here, present, copy = pieces[number]
        copy.wait()
        rows = staged.at[number]
        finish(rows, here, size)
        for n in range(out.shape[1] // TILE):
            cols = slice(n * TILE, (n + 1) * TILE)
            value = spread(table, rows, 0, size, present, n)
            out[:, cols] = value if entries is None else value + entries[:, cols]


def assemble_kernel(place, table, leaf, sep, upd, *refs):
    assemble(table, place[0], place[1], leaf, lambda rows, here, size: None, sep, upd, *refs)


def assembled_shapes(sep, upd, level):
    width = SEP if level == 3 else NF
    sep_shape = jax.ShapeDtypeStruct((sep.shape[0], SEP), jnp.float32)
    upd_shape = jax.ShapeDtypeStruct((upd.shape[0], width), jnp.float32)
    return [sep_shape, upd_shape, sep_shape, upd_shape]


def assemble_leaf(place, table, leaf, sep, upd):
    shapes = assembled_shapes(sep, upd, 1)
    return pl.pallas_call(
        assemble_kernel,
        out_shape=tuple(shapes),
        in_specs=[SCALARS] * 2 + [pl.BlockSpec(memory_space=pl.ANY)] + [WHOLE] * 2,
        out_specs=(WHOLE,) * 4,
        scratch_shapes=[pltpu.VMEM((4, upd.shape[0], UPD), jnp.float32), pltpu.SemaphoreType.DMA((4,))],
        compiler_params=pltpu.CompilerParams(vmem_limit_bytes=32 * 2**20),
    )(place, table, leaf, sep, upd)


def update_kernel(place, table, solved, rest, sep, upd, *refs):
    outs, (staged, sems, high, low) = refs[:4], refs[4:]
    high[...], low[...] = split(solved[...])

    def finish(rows, here, size):
        left = split(solved[pl.ds(here, size), :])
        rows[:size, :] = rows[:size, :] - dot3(left, (high[...], low[...]))

    assemble(table, place[0], place[1], rest, finish, sep, upd, *outs, staged, sems)


def update(place, table, solved, rest, sep, upd, level):
    shapes = assembled_shapes(sep, upd, level)
    return pl.pallas_call(
        update_kernel,
        out_shape=tuple(shapes),
        in_specs=[SCALARS] * 2 + [WHOLE, pl.BlockSpec(memory_space=pl.ANY), WHOLE, WHOLE],
        out_specs=(WHOLE,) * 4,
        scratch_shapes=[
            pltpu.VMEM((4, upd.shape[0], UPD), jnp.float32),
            pltpu.SemaphoreType.DMA((4,)),
            pltpu.VMEM((UPD, SEP), jnp.bfloat16),
            pltpu.VMEM((UPD, SEP), jnp.bfloat16),
        ],
        compiler_params=pltpu.CompilerParams(vmem_limit_bytes=40 * 2**20),
    )(place, table, solved, rest, sep, upd)


def bit_of(index, bit):
    return lax.rem(lax.div(index, jnp.int32(2**bit)), jnp.int32(2))


def front_dims(level, front_bits):
    return [("leaf", bit) for bit in range(level - 1, -1, -1)] + [("front", bit) for bit in range(front_bits - 1, -1, -1)]


def orders_of(level, front_bits):
    links = list(range(level + front_bits - 1))
    last = level + front_bits - 1
    if level == 3:
        swapped = links[:-2] + [links[-1], links[-2]]
        return [links + [last], swapped + [last]]
    return [links[turn:] + links[:turn] + [last] for turn in range(len(links))]


def column_parts(columns, parts):
    tiles = columns // TILE
    cuts = [round(tiles * part / parts) * TILE for part in range(parts + 1)]
    return [(cuts[part], cuts[part + 1] - cuts[part]) for part in range(parts)]


def partner_of(dim):
    axis, bit = dim
    index = lax.axis_index(axis)
    return {axis: index + (1 - 2 * bit_of(index, bit)) * 2**bit}


def doubling(buffer, dims, order, columns, send, recv):
    bits = [bit_of(lax.axis_index(axis), bit) for axis, bit in dims]
    copies = []
    for step, dim in enumerate(order):
        index = tuple(slice(None) if d in order[:step] else bits[d] for d in range(len(dims)))
        part = buffer.at[index + (slice(None), pl.ds(*columns))]
        copies.append(pltpu.make_async_remote_copy(
            src_ref=part,
            dst_ref=part,
            send_sem=send.at[step],
            recv_sem=recv.at[step],
            device_id=partner_of(dims[dim]),
            device_id_type=MESH,
        ))
    return copies


def level_kernel(level, front_bits, own_sep, own_upd, out_sep, out_upd, *refs):
    last = level == 3
    if last:
        diag, solved, below, full_solved, *refs = refs
    else:
        diag, solved, full_solved, f22, f21, *refs = refs
    f11, full_diag, work, inv, high, low, done_high, done_low, *refs = refs
    recv_sep, recv_upd, own_send, own_recv, all_send, all_recv = refs
    buffers = [f11] if last else [f11, f21, f22]
    dims = front_dims(level, front_bits)
    bits = [bit_of(lax.axis_index(axis), bit) for axis, bit in dims]
    steps = len(dims)
    position = lax.rem(lax.axis_index("leaf"), jnp.int32(2**level)) * 2**front_bits + lax.axis_index("front")

    barrier = pltpu.get_barrier_semaphore()
    for dim in dims:
        pl.semaphore_signal(barrier, inc=1, device_id=partner_of(dim), device_id_type=MESH)
    pl.semaphore_wait(barrier, steps)

    def to_sibling(src, dst, slot):
        return pltpu.make_async_remote_copy(
            src_ref=src, dst_ref=dst, send_sem=own_send.at[slot], recv_sem=own_recv.at[slot],
            device_id=partner_of(dims[0]), device_id_type=MESH)

    sep_copy = to_sibling(out_sep, recv_sep, 0)
    upd_copy = to_sibling(out_upd, recv_upd, 1)
    sep_copy.start()
    high[...] = jnp.zeros_like(high)
    low[...] = jnp.zeros_like(low)
    done_high[...] = jnp.zeros_like(done_high)
    done_low[...] = jnp.zeros_like(done_low)

    chains = []
    orders = orders_of(level, front_bits)
    blocks = SEP // TILE
    pieces = [(f11, (b * TILE, TILE), orders[b % len(orders)]) for b in range(blocks)]
    for buffer in buffers[1:]:
        pieces += [(buffer, columns, order) for columns, order in zip(column_parts(buffer.shape[-1], len(orders)), orders)]
    for slot, (buffer, columns, order) in enumerate(pieces):
        chains.append(doubling(buffer, dims, order, columns, all_send.at[slot], all_recv.at[slot]))
    early, late = chains[:blocks], chains[blocks:]
    own = tuple(bits)

    def advance(which, step):
        for chain in which:
            if step >= 0:
                chain[step].wait()
            if step + 1 < steps:
                chain[step + 1].start()

    sep_copy.wait()
    f11[own] = own_sep[...] + recv_sep[...]
    def skewed(turn):
        for b in range(blocks):
            if -1 <= turn - b < steps:
                advance(early[b:b + 1], turn - b)

    for turn in range(-1, steps):
        skewed(turn)
    upd_copy.start()

    def arrived():
        upd_copy.wait()
        if last:
            below[...] = own_upd[...] + recv_upd[...]
        else:
            f21[own] = own_upd[:, :SEP] + recv_upd[:, :SEP]
            f22[own] = own_upd[:, SEP:] + recv_upd[:, SEP:]
            advance(late, -1)

    flat = (slice(None),) * len(dims)

    @pl.loop(0, blocks)
    def _(b):
        pivot_block(b, lambda here: f11[flat + (slice(None), here)].reshape(SEP, TILE), full_diag, work, inv, high, low)

        for done in range(blocks - 1):
            @pl.when(b == done)
            def _():
                skewed(steps + done)

        @pl.when(b == 0)
        def _():
            arrived()

        if not last:
            for step in range(steps - 1):
                @pl.when(b == blocks - steps + 1 + step)
                def _():
                    advance(late, step)

    for chain in late[:len(orders)]:
        chain[steps - 1].wait()

    @pl.loop(0, blocks)
    def _(b):
        if last:
            piece = lambda here: below[:, here]
        else:
            piece = lambda here: f21[flat + (slice(None), here)].reshape(UPD, TILE)
        solve_block(b, piece, full_solved, inv, high, low, done_high, done_low)

    sep_count, upd_count = diag.shape[0], solved.shape[0]
    diag[...] = full_diag[pl.ds(pl.multiple_of(position * sep_count, 8), sep_count), :]
    if last:
        solved[...] = full_solved[...]
    else:
        solved[...] = full_solved[pl.ds(pl.multiple_of(position * upd_count, 8), upd_count), :]
    for chain in late[len(orders):]:
        chain[steps - 1].wait()


def factor_level(level, front_bits, own_sep, own_upd, out_sep, out_upd):
    last = level == 3
    sep_count, upd_count = own_sep.shape[0], own_upd.shape[0]
    lead = (2,) * (level + front_bits)
    steps = len(lead)
    rows = upd_count if last else UPD
    shapes = [(sep_count, SEP), (upd_count, SEP)]
    scratch = [(upd_count, SEP), (upd_count, SEP)] if last else [lead + (upd_count, SEP)]
    if not last:
        shapes += [(UPD, SEP), lead + (upd_count, UPD)]
    scratch += [lead + (sep_count, SEP), (SEP, SEP), (SEP, TILE), (SEP // TILE, TILE, TILE)]
    halves = [(SEP, SEP)] * 2 + [(rows, SEP)] * 2
    received = [own_sep.shape, own_upd.shape]
    chains = SEP // TILE + len(orders_of(level, front_bits)) * (0 if last else 2)
    return pl.pallas_call(
        functools.partial(level_kernel, level, front_bits),
        out_shape=tuple(jax.ShapeDtypeStruct(shape, jnp.float32) for shape in shapes),
        in_specs=[WHOLE] * 4,
        out_specs=(WHOLE,) * len(shapes),
        scratch_shapes=[pltpu.VMEM(shape, jnp.float32) for shape in scratch]
        + [pltpu.VMEM(shape, jnp.bfloat16) for shape in halves]
        + [pltpu.VMEM(shape, jnp.float32) for shape in received]
        + [
            pltpu.SemaphoreType.DMA((2,)),
            pltpu.SemaphoreType.DMA((2,)),
            pltpu.SemaphoreType.DMA((chains, steps)),
            pltpu.SemaphoreType.DMA((chains, steps)),
        ],
        compiler_params=pltpu.CompilerParams(
            collective_id=level, has_side_effects=True, vmem_limit_bytes=48 * 2**20),
    )(own_sep, own_upd, out_sep, out_upd)


def tile_table(tile_map):
    tiles = jnp.arange(NT, dtype=jnp.int32)
    match = tile_map[:, None] == tiles[None, :]
    place = jnp.sum(jnp.where(match, jnp.arange(UT, dtype=jnp.int32)[:, None], 0), axis=0)
    return jnp.concatenate([place, jnp.any(match, axis=0).astype(jnp.int32)])


def body(
    leaf_update,
    separator_rows_1,
    remaining_rows_1,
    separator_rows_2,
    remaining_rows_2,
    separator_rows_3,
    remaining_rows_3,
    child_map_1,
    child_map_2,
    child_map_3,
):
    leaf_place = lax.axis_index("leaf")
    front_place = lax.axis_index("front")
    front_count = lax.axis_size("front")
    front_bits = front_count.bit_length() - 1
    sections = (
        (separator_rows_1, remaining_rows_1, child_map_1),
        (separator_rows_2, remaining_rows_2, child_map_2),
        (separator_rows_3, remaining_rows_3, child_map_3),
    )
    tables = [
        tile_table(lax.dynamic_index_in_dim(maps, leaf_place >> number, 0, keepdims=False))
        for number, (_, _, maps) in enumerate(sections)
    ]
    positions = [
        (leaf_place % 2**level * front_count + front_place, (leaf_place ^ 1 << level - 1) % 2**level * front_count + front_place)
        for level in range(1, 4)
    ]
    results = []
    sep, upd, _ = sections[0]
    rows = assemble_leaf(jnp.stack(positions[0]).astype(jnp.int32), tables[0], leaf_update, sep, upd)
    for level in range(1, 4):
        outs = factor_level(level, front_bits, *rows)
        results += outs[:2]
        if level < 3:
            place = jnp.stack(positions[level]).astype(jnp.int32)
            sep, upd, _ = sections[level]
            rows = update(place, tables[level], outs[2], outs[3].reshape(UPD, UPD), sep, upd, level + 1)
    return tuple(results)


def solution(mesh):
    rows = P(("leaf", "front"), None)
    in_specs = (P("leaf", None),) + (rows,) * 6 + (P(),) * 3
    return jax.shard_map(body, mesh=mesh, in_specs=in_specs, out_specs=(rows,) * 6, check_vma=False)
```

```python
import functools

import jax
import jax.numpy as jnp
from jax import lax
from jax.experimental import pallas as pl
from jax.experimental.pallas import tpu as pltpu
from jax.sharding import PartitionSpec as P

TILE = 128
SEP = 512
UPD = 1024
NF = 1536
NT = 12
UT = 8
STRIP = 8
MESH = pl.DeviceIdType.MESH
WHOLE = pl.BlockSpec(memory_space=pltpu.VMEM)
SCALARS = pl.BlockSpec(memory_space=pltpu.SMEM)


def split(value):
    high = value.astype(jnp.bfloat16)
    return high, (value - high.astype(jnp.float32)).astype(jnp.bfloat16)


def dot3(left, right):
    def one(a, b):
        return lax.dot_general(a, b, (((1,), (1,)), ((), ())), preferred_element_type=jnp.float32)
    return one(left[0], right[0]) + (one(left[0], right[1]) + one(left[1], right[0]))


def invert_block(rows):
    count = len(rows)
    full = (STRIP, TILE)
    lane = lax.broadcasted_iota(jnp.int32, full, 1)
    sub = lax.broadcasted_iota(jnp.int32, full, 0)
    out = []
    for s in range(count):
        base = s * STRIP
        strip = rows[s]
        cols = [jnp.broadcast_to(strip[:, base + j:base + j + 1], full) for j in range(STRIP)]
        d = {(i, j): jnp.broadcast_to(cols[j][i:i + 1, :], full) for j in range(STRIP) for i in range(j, STRIP)}
        in_strip = (lane >= base) & (lane < base + STRIP)
        aug = jnp.where(in_strip, jnp.where(lane - base == sub, 1.0, 0.0), strip)
        x = [jnp.broadcast_to(aug[i:i + 1, :], full) for i in range(STRIP)]
        r = []
        for k in range(0, STRIP, 2):
            n = k + 1
            det = d[k, k] * d[n, n] - d[n, k] * d[n, k]
            r.append(lax.rsqrt(d[k, k]))
            r.append(d[k, k] * r[k] * lax.rsqrt(det))
            d[n, k] = d[n, k] * r[k]
            for i in range(k + 2, STRIP):
                d[i, k] = d[i, k] * r[k]
                d[i, n] = (d[i, n] - d[i, k] * d[n, k]) * r[n]
            for j in range(k + 2, STRIP):
                for i in range(j, STRIP):
                    d[i, j] = d[i, j] - (d[i, k] * d[j, k] + d[i, n] * d[j, n])
            x[k] = x[k] * r[k]
            x[n] = (x[n] - d[n, k] * x[k]) * r[n]
            for i in range(k + 2, STRIP):
                x[i] = x[i] - (d[i, k] * x[k] + d[i, n] * x[n])
        u = x[0]
        for k in range(1, STRIP):
            u = jnp.where(sub == k, x[k], u)
        out.append(jnp.where(lane < base + STRIP, u, 0.0))
        if s == count - 1:
            break
        v = list(x)
        for k in range(STRIP - 1, -1, -1):
            v[k] = v[k] * r[k]
            for i in range(k):
                v[i] = v[i] - d[k, i] * v[k]
        for t in range(s + 1, count):
            row = rows[t]
            new = jnp.where(in_strip, 0.0, row)
            for j in range(STRIP):
                new = new - jnp.broadcast_to(row[:, base + j:base + j + 1], full) * v[j]
            rows[t] = new
    return out


def pivot_block(b, pivot, diag, work, inv, high, low):
    start = pl.multiple_of(b * TILE, TILE)
    here = pl.ds(start, TILE)
    work[...] = pivot(here) - dot3((high[...], low[...]), (high[here, :], low[here, :]))
    strips = [work[pl.ds(pl.multiple_of(start + STRIP * t, STRIP), STRIP), :] for t in range(TILE // STRIP)]
    for t, strip in enumerate(invert_block(strips)):
        inv[b, STRIP * t:STRIP * t + STRIP, :] = strip
    column = dot3(split(work[...]), split(inv[b]))
    row_ids = lax.broadcasted_iota(jnp.int32, (SEP, TILE), 0)
    col_ids = lax.broadcasted_iota(jnp.int32, (SEP, TILE), 1) + start
    column = jnp.where(row_ids >= col_ids, column, 0.0)
    diag[:, here] = column
    high[:, here], low[:, here] = split(column)


def solve_block(b, below, solved, inv, high, low, done_high, done_low):
    here = pl.ds(pl.multiple_of(b * TILE, TILE), TILE)
    rest = below(here) - dot3((done_high[...], done_low[...]), (high[here, :], low[here, :]))
    column = dot3(split(rest), split(inv[b]))
    solved[:, here] = column
    done_high[:, here], done_low[:, here] = split(column)


def child_piece(table, row, count):
    tile = lax.div(row, jnp.int32(TILE))
    here = pl.multiple_of(table[tile] * TILE + lax.rem(row, jnp.int32(TILE)), 8)
    return here, table[NT + tile].astype(jnp.float32)


def spread(table, rows, here, count, present, n):
    there = pl.ds(pl.multiple_of(table[n] * TILE, TILE), TILE)
    return rows[pl.ds(here, count), there] * (present * table[NT + n].astype(jnp.float32))


def assemble(table, own, other, child_rows, sep, upd, own_sep, own_upd, out_sep, out_upd):
    for out, size, offset, place, entries in (
        (out_sep, sep.shape[0], 0, other, None),
        (own_sep, sep.shape[0], 0, own, sep),
        (out_upd, upd.shape[0], SEP, other, None),
        (own_upd, upd.shape[0], SEP, own, upd),
    ):
        here, present = child_piece(table, offset + place * size, size)
        rows, here = child_rows(here, size)
        for n in range(out.shape[1] // TILE):
            cols = slice(n * TILE, (n + 1) * TILE)
            value = spread(table, rows, here, size, present, n)
            out[:, cols] = value if entries is None else value + entries[:, cols]


def assemble_kernel(place, table, leaf, sep, upd, *outs):
    assemble(table, place[0], place[1], lambda here, size: (leaf, here), sep, upd, *outs)


def assembled_shapes(sep, upd, level):
    width = SEP if level == 3 else NF
    sep_shape = jax.ShapeDtypeStruct((sep.shape[0], SEP), jnp.float32)
    upd_shape = jax.ShapeDtypeStruct((upd.shape[0], width), jnp.float32)
    return [sep_shape, upd_shape, sep_shape, upd_shape]


def assemble_leaf(place, table, leaf, sep, upd):
    shapes = assembled_shapes(sep, upd, 1)
    return pl.pallas_call(
        assemble_kernel,
        out_shape=tuple(shapes),
        in_specs=[SCALARS] * 2 + [WHOLE] * 3,
        out_specs=(WHOLE,) * 4,
        compiler_params=pltpu.CompilerParams(vmem_limit_bytes=32 * 2**20),
    )(place, table, leaf, sep, upd)


def update_kernel(place, table, solved, rest, sep, upd, *refs):
    outs, (high, low, child) = refs[:4], refs[4:]
    high[...], low[...] = split(solved[...])

    def update_rows(here, size):
        left = split(solved[pl.ds(here, size), :])
        child[:size, :] = rest[pl.ds(here, size), :] - dot3(left, (high[...], low[...]))
        return child, 0

    assemble(table, place[0], place[1], update_rows, sep, upd, *outs)


def update(place, table, solved, rest, sep, upd, level):
    shapes = assembled_shapes(sep, upd, level)
    return pl.pallas_call(
        update_kernel,
        out_shape=tuple(shapes),
        in_specs=[SCALARS] * 2 + [WHOLE] * 4,
        out_specs=(WHOLE,) * 4,
        scratch_shapes=[
            pltpu.VMEM((UPD, SEP), jnp.bfloat16),
            pltpu.VMEM((UPD, SEP), jnp.bfloat16),
            pltpu.VMEM((upd.shape[0], UPD), jnp.float32),
        ],
        compiler_params=pltpu.CompilerParams(vmem_limit_bytes=40 * 2**20),
    )(place, table, solved, rest, sep, upd)


def bit_of(index, bit):
    return lax.rem(lax.div(index, jnp.int32(2**bit)), jnp.int32(2))


def front_dims(level, front_bits):
    return [("leaf", bit) for bit in range(level - 1, -1, -1)] + [("front", bit) for bit in range(front_bits - 1, -1, -1)]


def orders_of(level, front_bits):
    links = list(range(level + front_bits - 1))
    last = level + front_bits - 1
    if level == 3:
        swapped = links[:-2] + [links[-1], links[-2]]
        return [links + [last], swapped + [last]]
    return [links[turn:] + links[:turn] + [last] for turn in range(len(links))]


def column_parts(columns, parts):
    tiles = columns // TILE
    cuts = [round(tiles * part / parts) * TILE for part in range(parts + 1)]
    return [(cuts[part], cuts[part + 1] - cuts[part]) for part in range(parts)]


def partner_of(dim):
    axis, bit = dim
    index = lax.axis_index(axis)
    return {axis: index + (1 - 2 * bit_of(index, bit)) * 2**bit}


def doubling(buffer, dims, order, columns, send, recv):
    bits = [bit_of(lax.axis_index(axis), bit) for axis, bit in dims]
    copies = []
    for step, dim in enumerate(order):
        index = tuple(slice(None) if d in order[:step] else bits[d] for d in range(len(dims)))
        part = buffer.at[index + (slice(None), pl.ds(*columns))]
        copies.append(pltpu.make_async_remote_copy(
            src_ref=part,
            dst_ref=part,
            send_sem=send.at[step],
            recv_sem=recv.at[step],
            device_id=partner_of(dims[dim]),
            device_id_type=MESH,
        ))
    return copies


def level_kernel(level, front_bits, own_sep, own_upd, out_sep, out_upd, *refs):
    last = level == 3
    if last:
        diag, solved, below, full_solved, *refs = refs
    else:
        diag, solved, full_solved, f22, f21, *refs = refs
    f11, full_diag, work, inv, high, low, done_high, done_low, *refs = refs
    recv_sep, recv_upd, own_send, own_recv, all_send, all_recv = refs
    buffers = [f11] if last else [f11, f21, f22]
    dims = front_dims(level, front_bits)
    bits = [bit_of(lax.axis_index(axis), bit) for axis, bit in dims]
    steps = len(dims)
    position = lax.rem(lax.axis_index("leaf"), jnp.int32(2**level)) * 2**front_bits + lax.axis_index("front")

    barrier = pltpu.get_barrier_semaphore()
    for dim in dims:
        pl.semaphore_signal(barrier, inc=1, device_id=partner_of(dim), device_id_type=MESH)
    pl.semaphore_wait(barrier, steps)

    def to_sibling(src, dst, slot):
        return pltpu.make_async_remote_copy(
            src_ref=src, dst_ref=dst, send_sem=own_send.at[slot], recv_sem=own_recv.at[slot],
            device_id=partner_of(dims[0]), device_id_type=MESH)

    sep_copy = to_sibling(out_sep, recv_sep, 0)
    upd_copy = to_sibling(out_upd, recv_upd, 1)
    sep_copy.start()
    if last:
        upd_copy.start()
    high[...] = jnp.zeros_like(high)
    low[...] = jnp.zeros_like(low)
    done_high[...] = jnp.zeros_like(done_high)
    done_low[...] = jnp.zeros_like(done_low)

    chains = []
    orders = orders_of(level, front_bits)
    for item, buffer in enumerate(buffers):
        parts = column_parts(buffer.shape[-1], len(orders))
        if level == 1 and item > 0:
            head = buffer.shape[-1] * 3 // 4
            parts = [(0, head), (head, buffer.shape[-1] - head)]
        for part, columns in enumerate(parts):
            slot = item * len(orders) + part
            chains.append(doubling(buffer, dims, orders[part], columns, all_send.at[slot], all_recv.at[slot]))
    early, late = chains[:len(orders)], chains[len(orders):]
    own = tuple(bits)

    def advance(which, step):
        for chain in which:
            if step >= 0:
                chain[step].wait()
            if step + 1 < steps:
                chain[step + 1].start()

    sep_copy.wait()
    f11[own] = own_sep[...] + recv_sep[...]
    advance(early, -1)
    for step in range(steps):
        if step == steps - 1 and not last:
            upd_copy.start()
        advance(early, step)

    def arrived():
        upd_copy.wait()
        if last:
            below[...] = own_upd[...] + recv_upd[...]
        else:
            f21[own] = own_upd[:, :SEP] + recv_upd[:, :SEP]
            f22[own] = own_upd[:, SEP:] + recv_upd[:, SEP:]
            advance(late, -1)

    blocks = SEP // TILE
    flat = (slice(None),) * len(dims)

    def next_pivot(b):
        pivot_block(b, lambda here: f11[flat + (slice(None), here)].reshape(SEP, TILE), full_diag, work, inv, high, low)

    def next_solve(b):
        if last:
            piece = lambda here: below[:, here]
        else:
            piece = lambda here: f21[flat + (slice(None), here)].reshape(UPD, TILE)
        solve_block(b, piece, full_solved, inv, high, low, done_high, done_low)

    if last:
        arrived()

        @pl.loop(0, blocks)
        def _(b):
            next_pivot(b)
            next_solve(b)
    else:
        @pl.loop(0, blocks)
        def _(b):
            next_pivot(b)

            @pl.when(b == 0)
            def _():
                arrived()

            for step in range(steps - 1):
                @pl.when(b == blocks - steps + 1 + step)
                def _():
                    advance(late, step)

        for chain in late[:len(orders)]:
            chain[steps - 1].wait()

        @pl.loop(0, blocks)
        def _(b):
            next_solve(b)

    sep_count, upd_count = diag.shape[0], solved.shape[0]
    diag[...] = full_diag[pl.ds(pl.multiple_of(position * sep_count, 8), sep_count), :]
    if last:
        solved[...] = full_solved[...]
    else:
        solved[...] = full_solved[pl.ds(pl.multiple_of(position * upd_count, 8), upd_count), :]
    for chain in late[len(orders):]:
        chain[steps - 1].wait()


def factor_level(level, front_bits, own_sep, own_upd, out_sep, out_upd):
    last = level == 3
    sep_count, upd_count = own_sep.shape[0], own_upd.shape[0]
    lead = (2,) * (level + front_bits)
    steps = len(lead)
    rows = upd_count if last else UPD
    shapes = [(sep_count, SEP), (upd_count, SEP)]
    scratch = [(upd_count, SEP), (upd_count, SEP)] if last else [lead + (upd_count, SEP)]
    if not last:
        shapes += [(UPD, SEP), lead + (upd_count, UPD)]
    scratch += [lead + (sep_count, SEP), (SEP, SEP), (SEP, TILE), (SEP // TILE, TILE, TILE)]
    halves = [(SEP, SEP)] * 2 + [(rows, SEP)] * 2
    received = [own_sep.shape, own_upd.shape]
    chains = len(orders_of(level, front_bits)) * (1 if last else 3)
    return pl.pallas_call(
        functools.partial(level_kernel, level, front_bits),
        out_shape=tuple(jax.ShapeDtypeStruct(shape, jnp.float32) for shape in shapes),
        in_specs=[WHOLE] * 4,
        out_specs=(WHOLE,) * len(shapes),
        scratch_shapes=[pltpu.VMEM(shape, jnp.float32) for shape in scratch]
        + [pltpu.VMEM(shape, jnp.bfloat16) for shape in halves]
        + [pltpu.VMEM(shape, jnp.float32) for shape in received]
        + [
            pltpu.SemaphoreType.DMA((2,)),
            pltpu.SemaphoreType.DMA((2,)),
            pltpu.SemaphoreType.DMA((chains, steps)),
            pltpu.SemaphoreType.DMA((chains, steps)),
        ],
        compiler_params=pltpu.CompilerParams(
            collective_id=level, has_side_effects=True, vmem_limit_bytes=48 * 2**20),
    )(own_sep, own_upd, out_sep, out_upd)


def tile_table(tile_map):
    tiles = jnp.arange(NT, dtype=jnp.int32)
    match = tile_map[:, None] == tiles[None, :]
    place = jnp.sum(jnp.where(match, jnp.arange(UT, dtype=jnp.int32)[:, None], 0), axis=0)
    return jnp.concatenate([place, jnp.any(match, axis=0).astype(jnp.int32)])


def body(
    leaf_update,
    separator_rows_1,
    remaining_rows_1,
    separator_rows_2,
    remaining_rows_2,
    separator_rows_3,
    remaining_rows_3,
    child_map_1,
    child_map_2,
    child_map_3,
):
    leaf_place = lax.axis_index("leaf")
    front_place = lax.axis_index("front")
    front_count = lax.axis_size("front")
    front_bits = front_count.bit_length() - 1
    sections = (
        (separator_rows_1, remaining_rows_1, child_map_1),
        (separator_rows_2, remaining_rows_2, child_map_2),
        (separator_rows_3, remaining_rows_3, child_map_3),
    )
    tables = [
        tile_table(lax.dynamic_index_in_dim(maps, leaf_place >> number, 0, keepdims=False))
        for number, (_, _, maps) in enumerate(sections)
    ]
    positions = [
        (leaf_place % 2**level * front_count + front_place, (leaf_place ^ 1 << level - 1) % 2**level * front_count + front_place)
        for level in range(1, 4)
    ]
    results = []
    sep, upd, _ = sections[0]
    rows = assemble_leaf(jnp.stack(positions[0]).astype(jnp.int32), tables[0], leaf_update, sep, upd)
    for level in range(1, 4):
        outs = factor_level(level, front_bits, *rows)
        results += outs[:2]
        if level < 3:
            place = jnp.stack(positions[level]).astype(jnp.int32)
            sep, upd, _ = sections[level]
            rows = update(place, tables[level], outs[2], outs[3].reshape(UPD, UPD), sep, upd, level + 1)
    return tuple(results)


def solution(mesh):
    rows = P(("leaf", "front"), None)
    in_specs = (P("leaf", None),) + (rows,) * 6 + (P(),) * 3
    return jax.shard_map(body, mesh=mesh, in_specs=in_specs, out_specs=(rows,) * 6, check_vma=False)
```
